32 devices in a mesh: depth: 16 (over z, y, core), filt: 2 (over x).
Axes of the slice: x: 2, y: 2, z: 4, core: 2. Of those that a mesh axis runs over, the one named last changes fastest.
Arguments:
- volume: bfloat16 [128, 16, 1024], P('filt', 'depth'), may hold values from -6 to 6
- up_weight: bfloat16 [128, 4096], P(None, 'filt'), may hold values from -0.1875 to 0.1875
- up_bias: float32 [64], P('filt'), may hold values from -3 to 3
- first_weight: bfloat16 [27, 4096], replicated, may hold values from -0.15625 to 0.15625
- first_bias: float32 [64], replicated, may hold values from -3 to 3
- second_weight: bfloat16 [27, 4096], replicated, may hold values from -0.15625 to 0.15625
- second_bias: float32 [64], replicated, may hold values from -3 to 3
Outputs:
- decoded: bfloat16 [64, 32, 32, 128], P('filt', 'depth')
The draws below stay inside these ranges and needn't reach their ends.
All inputs are finite; a program needn't handle non-finite values.
Results may differ from the reference program's by a relative error of at most 0.0052.
Values may be sent and summed in bfloat16 or wider, within the bound.
A program may use at most 64 MiB of HBM per device.

```python
import jax
import jax.numpy as jnp
from jax import lax

C_IN = 128
C_OUT = 64
IN_H = 16
IN_HW = 64
IN_DEPTH = 16


def level_of(own_key, shape, cuts, smallest, top_value):
    def one(axis_at, blocks):
        draws = jax.random.uniform(jax.random.fold_in(jax.random.fold_in(own_key, 6), axis_at), (blocks,), jnp.float32, smallest / len(cuts), top_value / len(cuts))
        return jnp.repeat(jnp.exp(draws), shape[axis_at] // blocks).reshape((-1,) + (1,) * (len(shape) - axis_at - 1))

    factor_of = one(*cuts[0])
    for cut in cuts[1:]:
        factor_of = factor_of * one(*cut)
    return factor_of


def scatter_about(key, extent, width, most, pieces=(), kind=jnp.bfloat16):
    drawn = width * jax.random.normal(key, extent, jnp.float32)
    if pieces:
        drawn = drawn * level_of(key, extent, pieces, -0.22, 0.18)
    return jnp.clip(drawn, -most, most).astype(kind)


def setup_inputs(seed: int = 0) -> dict:
    seeds = jax.random.split(jax.random.key(seed), 8)
    return {
        "volume": scatter_about(seeds[0], (C_IN, IN_DEPTH, IN_H * IN_HW), 1.0, 6.0, ((0, 2), (1, 16))),
        "up_weight": scatter_about(seeds[1], (C_IN, C_OUT * 64), (C_IN * 8) ** -0.5, 0.1875, ((1, 2),)),
        "up_bias": scatter_about(seeds[2], (C_OUT,), 0.5, 3.0, ((0, 2),), jnp.float32),
        "first_weight": scatter_about(seeds[3], (27, C_OUT * C_OUT), (C_OUT * 27) ** -0.5, 0.15625),
        "first_bias": scatter_about(seeds[4], (C_OUT,), 0.5, 3.0, (), jnp.float32),
        "second_weight": scatter_about(seeds[5], (27, C_OUT * C_OUT), (C_OUT * 27) ** -0.5, 0.15625),
        "second_bias": scatter_about(seeds[6], (C_OUT,), 0.5, 3.0, (), jnp.float32),
    }


def upsample(padded, weight):
    kernel = jnp.transpose(weight, (1, 0, 2, 3, 4))
    count_d = padded.shape[1] - 2
    count_h = padded.shape[2] - 2
    count_w = padded.shape[3] - 2
    results = []
    for phase_d in range(2):
        for phase_h in range(2):
            for phase_w in range(2):
                taps = kernel[:, :, 3 - phase_d::-2, 3 - phase_h::-2, 3 - phase_w::-2]
                window = padded[:, phase_d:phase_d + count_d + 1, phase_h:phase_h + count_h + 1, phase_w:phase_w + count_w + 1]
                result = lax.conv_general_dilated(window[None], taps, (1, 1, 1), "VALID", dimension_numbers=("NCDHW", "OIDHW", "NCDHW"), preferred_element_type=jnp.float32)[0]
                results.append(result)
    stacked = jnp.stack(results).reshape((2, 2, 2) + results[0].shape)
    stacked = jnp.transpose(stacked, (3, 4, 0, 5, 1, 6, 2))
    return stacked.reshape(stacked.shape[0], 2 * count_d, 2 * count_h, 2 * count_w)


def unpack_conv(weight):
    return jnp.transpose(weight.reshape(3, 3, 3, C_OUT, C_OUT), (3, 4, 0, 1, 2))


def convolve(activation, weight):
    return lax.conv_general_dilated(activation[None], weight, (1, 1, 1), ((1, 1), (1, 1), (1, 1)), dimension_numbers=("NCDHW", "OIDHW", "NCDHW"), preferred_element_type=jnp.float32)[0]


def leaky(value):
    return jnp.where(value > 0, value, 0.2 * value)


def reference(volume, up_weight, up_bias, first_weight, first_bias, second_weight, second_bias):
    cube = volume.reshape(volume.shape[0], volume.shape[1], IN_H, IN_HW)
    up_kernel = up_weight.reshape(up_weight.shape[0], C_OUT, 4, 4, 4)
    padded = jnp.pad(cube, ((0, 0), (1, 1), (1, 1), (1, 1)))
    upsampled = (upsample(padded, up_kernel) + up_bias[:, None, None, None]).astype(jnp.bfloat16)
    hidden = leaky(convolve(upsampled, unpack_conv(first_weight)) + first_bias[:, None, None, None]).astype(jnp.bfloat16)
    decoded = leaky(convolve(hidden, unpack_conv(second_weight)) + second_bias[:, None, None, None]).astype(jnp.bfloat16)
    return decoded
```

```python
import functools

import jax
import jax.numpy as jnp
from jax import lax
from jax.experimental import pallas as pl
from jax.experimental.pallas import tpu as pltpu
from jax.sharding import PartitionSpec as P

BF = jnp.bfloat16
F32 = jnp.float32
MESH = pl.DeviceIdType.MESH


def shift_add(low, mid, high, lane):
    left = jnp.where(lane > 0, pltpu.roll(low, 1, 1), 0.0)
    right = jnp.where(lane < 127, pltpu.roll(high, 127, 1), 0.0)
    return mid + left + right


def conv_rows(src, weight, bias, plane, row, count, lane):
    parts = []
    for kd in range(3):
        for kh in range(3):
            rows = [src[plane + kd, row + kh + r] for r in range(count)]
            parts.append(jnp.concatenate(rows, axis=1))
    stacked = jnp.concatenate(parts, axis=0)
    total = jnp.dot(weight, stacked, preferred_element_type=F32)
    outs = []
    for r in range(count):
        cols = slice(128 * r, 128 * r + 128)
        value = shift_add(total[0:64, cols], total[64:128, cols], total[128:192, cols], lane)
        value = value + bias
        outs.append(jnp.maximum(value, 0.2 * value))
    return outs


def kernel(devices, vol, wt, w1, w2, bu, b1, b2, out,
           grid_in, moved, wup, ups, hid, result,
           send, recv, xsend, wsend, wrecv, osend, orecv, lsem):
    d = lax.axis_index("depth")
    f = lax.axis_index("filt")
    g = 1 - f
    core = lax.rem(d, 2)
    s = 1 - 2 * core

    def exists(t):
        return jnp.logical_and(t >= 0, t < devices)

    barrier = pltpu.get_barrier_semaphore()
    pl.semaphore_signal(barrier, inc=1, device_id=(d, g), device_id_type=MESH)
    for off in (-2, -1, 1, 2):
        @pl.when(exists(d + off))
        def _():
            pl.semaphore_signal(barrier, inc=1, device_id=(d + off, f), device_id_type=MESH)
    peers = 1
    for off in (-2, -1, 1, 2):
        peers = peers + jnp.where(exists(d + off), 1, 0)
    pl.semaphore_wait(barrier, peers)

    x_copy = pltpu.make_async_remote_copy(
        src_ref=vol.at[:, pl.ds(pl.multiple_of(384 * g, 128), 640)],
        dst_ref=grid_in.at[2, f], send_sem=xsend, recv_sem=recv.at[2, f],
        device_id=(d, g), device_id_type=MESH)
    x_copy.start()
    w_half = pl.ds(8 * core, 8)
    w_copy = pltpu.make_async_remote_copy(
        src_ref=wt.at[w_half], dst_ref=wup.at[w_half, f], send_sem=wsend.at[0], recv_sem=wrecv.at[0],
        device_id=(d, g), device_id_type=MESH)
    w_copy.start()
    grid_in[2, f] = vol[:, pl.ds(pl.multiple_of(384 * f, 128), 640)]

    def to_depth(half, which, at, target):
        slot = d - target + 2 if which < 3 else 2 - 2 * s
        return pltpu.make_async_remote_copy(
            src_ref=grid_in.at[at, half], dst_ref=grid_in.at[slot, half],
            send_sem=send.at[which, half], recv_sem=recv.at[slot, half],
            device_id=(target, f), device_id_type=MESH)

    def arrived(slot, half):
        pltpu.make_async_copy(grid_in.at[slot, half], grid_in.at[slot, half], recv.at[slot, half]).wait()

    def start_half(half):
        for which, off in enumerate((-s, s, 2 * s)):
            @pl.when(exists(d + off))
            def _():
                to_depth(half, which, 2, d + off).start()

    start_half(f)
    for off in (-2, -1, 1, 2):
        @pl.when(jnp.logical_not(exists(d + off)))
        def _():
            grid_in[2 + off] = jnp.zeros(grid_in.shape[1:], BF)
    for k in range(16):
        wup[k, f] = wt[k]
    ups[:, 0] = jnp.zeros((6, 64, 128), BF)
    ups[:, 21] = jnp.zeros((6, 64, 128), BF)
    hid[:, 0] = jnp.zeros((4, 64, 128), BF)
    hid[:, 19] = jnp.zeros((4, 64, 128), BF)

    x_recv = pltpu.make_async_copy(grid_in.at[2, g], grid_in.at[2, g], recv.at[2, g])
    x_recv.wait()
    start_half(g)

    def forward(half):
        @pl.when(exists(d - s))
        def _():
            arrived(2 - s, half)
            to_depth(half, 3, 2 - s, d + s).start()

    forward(f)
    w_other = pl.ds(8 * (1 - core), 8)
    w_copy.wait_recv()
    w_forward = pltpu.make_async_remote_copy(
        src_ref=wup.at[w_half, g], dst_ref=wup.at[w_half, g], send_sem=wsend.at[1], recv_sem=wrecv.at[1],
        device_id=(d + s, f), device_id_type=MESH)
    w_forward.start()
    forward(g)
    for half in range(2):
        arrived(2 + s, half)
    w_forward.wait_recv()

    lane = lax.broadcasted_iota(jnp.int32, (64, 128), 1)
    lane_in = lax.broadcasted_iota(jnp.int32, (128, 128), 1)
    row_at = lax.broadcasted_iota(jnp.int32, (256, 256), 0)
    col_at = lax.broadcasted_iota(jnp.int32, (256, 256), 1)
    odd, rest = row_at // 128, row_at % 128
    place = jnp.where(col_at == 128 * (rest // 64) + 2 * (rest % 64) + odd, 1.0, 0.0).astype(BF)
    bias_up, bias_1, bias_2 = bu[...], b1[...], b2[...]

    def shifted(slot):
        whole = grid_in[slot].reshape(128, 640).astype(F32)
        zero = jnp.zeros((128, 128), F32)
        turned = [zero] + [pltpu.roll(whole[:, 128 * t:128 * t + 128], 64, 1) for t in range(5)] + [zero]
        for t in range(6):
            moved[slot, :, 128 * t:128 * t + 128] = jnp.where(lane_in < 64, turned[t], turned[t + 1]).astype(BF)

    def upsample_plane(p):
        q, pd = p // 2, p % 2
        inside = exists(d - 1 + q)
        slots = (q + 1, q + 2 * pd)
        kds = (1 + pd, 3 - 3 * pd)
        for ph in range(2):
            khs = (1 + ph, 3 - 3 * ph)
            left, right = [], []
            for slot, kd in zip(slots, kds):
                for at, kh in enumerate(khs):
                    left.append(wup[4 * kd + kh].reshape(256, 128))
                    if at == 0:
                        right.append(grid_in[slot].reshape(128, 640))
                    else:
                        right.append(moved[slot, :, 128 * ph:128 * ph + 640])
            total = jnp.dot(jnp.concatenate(left, axis=1), jnp.concatenate(right, axis=0),
                            preferred_element_type=F32)
            rows = []
            for t in range(5):
                cols = slice(128 * t, 128 * t + 128)
                tap = [jnp.concatenate([total[32 * k:32 * k + 32, cols], total[128 + 32 * k:160 + 32 * k, cols]], axis=0)
                       for k in range(4)]
                even = tap[1] + jnp.where(lane % 64 > 0, pltpu.roll(tap[3], 1, 1), 0.0) + bias_up
                odd_ = tap[2] + jnp.where(lane % 64 < 63, pltpu.roll(tap[0], 127, 1), 0.0) + bias_up
                rows.append(jnp.concatenate([even, odd_], axis=1))
            both = jnp.where(inside, jnp.concatenate(rows, axis=0), 0.0).astype(BF)
            mixed = jnp.dot(both, place, preferred_element_type=F32).astype(BF)
            for t in range(5):
                for r in range(2):
                    ups[p, 1 + 2 * (2 * t + r) + ph] = mixed[64 * t:64 * t + 64, 128 * r:128 * r + 128]

    for slot in (1, 2, 3):
        shifted(slot)
    lax.fori_loop(1, 5, lambda p, c: (upsample_plane(p), c)[1], 0)

    for half in range(2):
        @pl.when(exists(d - 2 * s))
        def _():
            arrived(2 - 2 * s, half)

        @pl.when(exists(d + 2 * s))
        def _():
            arrived(2 + 2 * s, half)
    for slot in (0, 4):
        shifted(slot)
    lax.fori_loop(0, 2, lambda i, c: (upsample_plane(5 * i), c)[1], 0)

    first, second = w1[...], w2[...]

    def hidden_step(i, c):
        plane, row = i // 3, 6 * (i % 3)
        at = 2 * d - 1 + plane
        inside = jnp.logical_and(at >= 0, at < 2 * devices)
        for r, value in enumerate(conv_rows(ups, first, bias_1, plane, 2 * f + row, 6, lane)):
            hid[plane, 1 + row + r] = jnp.where(inside, value, 0.0).astype(BF)
        return c

    lax.fori_loop(0, 12, hidden_step, 0)

    rows_mine = pl.ds(16 * f, 16)

    def out_copy(plane):
        return pltpu.make_async_remote_copy(
            src_ref=result.at[plane, g], dst_ref=out.at[plane, rows_mine],
            send_sem=osend.at[plane], recv_sem=orecv.at[plane], device_id=(d, g), device_id_type=MESH)

    def own_copy(plane):
        return pltpu.make_async_copy(result.at[plane, f], out.at[plane, rows_mine], lsem.at[plane])

    for plane in range(2):
        def step(i, c):
            row = 4 * i
            for r, value in enumerate(conv_rows(hid, second, bias_2, plane, 2 * f + row, 4, lane)):
                value = value.astype(BF)
                result[plane, 0, row + r] = value[0:32]
                result[plane, 1, row + r] = value[32:64]
            return c

        lax.fori_loop(0, 4, step, 0)
        out_copy(plane).start()
        own_copy(plane).start()

    x_copy.wait_send()
    w_copy.wait_send()
    w_forward.wait_send()
    for half in range(2):
        for which, off in enumerate((-s, s, 2 * s)):
            @pl.when(exists(d + off))
            def _():
                to_depth(half, which, 2, d + off).wait_send()

        @pl.when(exists(d - s))
        def _():
            to_depth(half, 3, 2 - s, d + s).wait_send()
    for plane in range(2):
        own_copy(plane).wait()
        out_copy(plane).wait()


def shards(devices, volume, up_weight, up_bias, first_weight, first_bias, second_weight, second_bias):
    vol = volume.reshape(64, 1024)
    wt = jnp.transpose(up_weight.reshape(128, 32, 16, 4), (2, 3, 1, 0)).reshape(16, 128, 128)
    bias_up = lax.all_gather(up_bias, "filt", axis=0, tiled=True)

    def taps(weight):
        return jnp.transpose(weight.reshape(9, 3, 64, 64), (1, 2, 0, 3)).reshape(192, 576)

    vmem = pl.BlockSpec(memory_space=pltpu.VMEM)
    out = pl.pallas_call(
        functools.partial(kernel, devices),
        out_shape=jax.ShapeDtypeStruct((2, 32, 32, 128), BF),
        in_specs=[vmem] * 7,
        out_specs=vmem,
        scratch_shapes=[
            pltpu.VMEM((5, 2, 64, 640), BF),
            pltpu.VMEM((5, 128, 768), BF),
            pltpu.VMEM((16, 2, 128, 128), BF),
            pltpu.VMEM((6, 22, 64, 128), BF),
            pltpu.VMEM((4, 20, 64, 128), BF),
            pltpu.VMEM((2, 2, 16, 32, 128), BF),
            pltpu.SemaphoreType.DMA((4, 2)),
            pltpu.SemaphoreType.DMA((5, 2)),
            pltpu.SemaphoreType.DMA,
            pltpu.SemaphoreType.DMA((2,)),
            pltpu.SemaphoreType.DMA((2,)),
            pltpu.SemaphoreType.DMA((2,)),
            pltpu.SemaphoreType.DMA((2,)),
            pltpu.SemaphoreType.DMA((2,)),
        ],
        compiler_params=pltpu.CompilerParams(
            collective_id=0, has_side_effects=True, vmem_limit_bytes=48 * 1024 * 1024),
    )(vol, wt, taps(first_weight), taps(second_weight), bias_up[:, None], first_bias[:, None], second_bias[:, None])
    return jnp.transpose(out, (2, 0, 1, 3))


def solution(mesh):
    placed = (P("filt", "depth", None), P(None, "filt"), P("filt"), P(), P(), P(), P())
    return jax.shard_map(
        functools.partial(shards, mesh.shape["depth"]),
        mesh=mesh,
        in_specs=placed,
        out_specs=P("filt", "depth", None, None),
        check_vma=False,
    )
```

```python
import functools

import jax
import jax.numpy as jnp
from jax import lax
from jax.experimental import pallas as pl
from jax.experimental.pallas import tpu as pltpu
from jax.sharding import PartitionSpec as P

BF = jnp.bfloat16
F32 = jnp.float32
MESH = pl.DeviceIdType.MESH


def shift_add(low, mid, high, lane):
    left = jnp.where(lane > 0, pltpu.roll(low, 1, 1), 0.0)
    right = jnp.where(lane < 127, pltpu.roll(high, 127, 1), 0.0)
    return mid + left + right


def conv_rows(src, weight, bias, plane, row, count, lane):
    parts = []
    for kd in range(3):
        for kh in range(3):
            rows = [src[plane + kd, row + kh + r] for r in range(count)]
            parts.append(jnp.concatenate(rows, axis=1))
    stacked = jnp.concatenate(parts, axis=0)
    total = jnp.dot(weight, stacked, preferred_element_type=F32)
    outs = []
    for r in range(count):
        cols = slice(128 * r, 128 * r + 128)
        value = shift_add(total[0:64, cols], total[64:128, cols], total[128:192, cols], lane)
        value = value + bias
        outs.append(jnp.maximum(value, 0.2 * value))
    return outs


def kernel(devices, vol, wt, w1, w2, bu, b1, b2, out,
           grid_in, moved, wup, ups, hid, result, bmine, bother, spread, packed, wconv,
           send, recv, xsend, wsend, wrecv, osend, orecv, lsem, bsem):
    d = lax.axis_index("depth")
    f = lax.axis_index("filt")
    g = 1 - f
    core = lax.rem(d, 2)
    s = 1 - 2 * core

    def exists(t):
        return jnp.logical_and(t >= 0, t < devices)

    barrier = pltpu.get_barrier_semaphore()
    pl.semaphore_signal(barrier, inc=1, device_id=(d, g), device_id_type=MESH)
    for off in (-2, -1, 1, 2):
        @pl.when(exists(d + off))
        def _():
            pl.semaphore_signal(barrier, inc=1, device_id=(d + off, f), device_id_type=MESH)
    peers = 1
    for off in (-2, -1, 1, 2):
        peers = peers + jnp.where(exists(d + off), 1, 0)
    pl.semaphore_wait(barrier, peers)

    x_copy = pltpu.make_async_remote_copy(
        src_ref=vol.at[:, pl.ds(pl.multiple_of(384 * g, 128), 640)],
        dst_ref=grid_in.at[2, f], send_sem=xsend, recv_sem=recv.at[2, f],
        device_id=(d, g), device_id_type=MESH)
    x_copy.start()
    w_half = pl.ds(8 * core, 8)
    w_copy = pltpu.make_async_remote_copy(
        src_ref=wt.at[w_half], dst_ref=wup.at[w_half, f], send_sem=wsend.at[0], recv_sem=wrecv.at[0],
        device_id=(d, g), device_id_type=MESH)
    w_copy.start()
    bmine[...] = jnp.zeros((8, 128), F32)
    bmine[0:1, 0:32] = bu[...]
    b_copy = pltpu.make_async_remote_copy(
        src_ref=bmine, dst_ref=bother, send_sem=bsem.at[0], recv_sem=bsem.at[1],
        device_id=(d, g), device_id_type=MESH)
    b_copy.start()
    grid_in[2, f] = vol[:, pl.ds(pl.multiple_of(384 * f, 128), 640)]

    def to_depth(half, which, at, target):
        slot = d - target + 2 if which < 3 else 2 - 2 * s
        return pltpu.make_async_remote_copy(
            src_ref=grid_in.at[at, half], dst_ref=grid_in.at[slot, half],
            send_sem=send.at[which, half], recv_sem=recv.at[slot, half],
            device_id=(target, f), device_id_type=MESH)

    def arrived(slot, half):
        pltpu.make_async_copy(grid_in.at[slot, half], grid_in.at[slot, half], recv.at[slot, half]).wait()

    def start_half(half, some):
        for which in some:
            off = (-s, s, 2 * s)[which]

            @pl.when(exists(d + off))
            def _():
                to_depth(half, which, 2, d + off).start()

    start_half(f, (0, 1))
    for off in (-2, -1, 1, 2):
        @pl.when(jnp.logical_not(exists(d + off)))
        def _():
            grid_in[2 + off] = jnp.zeros(grid_in.shape[1:], BF)
    for k in range(16):
        wup[k, f] = wt[k]
    ups[:, 0] = jnp.zeros((6, 64, 128), BF)
    ups[:, 21] = jnp.zeros((6, 64, 128), BF)
    hid[:, 0] = jnp.zeros((4, 64, 128), BF)
    hid[:, 19] = jnp.zeros((4, 64, 128), BF)

    x_recv = pltpu.make_async_copy(grid_in.at[2, g], grid_in.at[2, g], recv.at[2, g])
    x_recv.wait()
    start_half(g, (0, 1))
    start_half(f, (2,))
    start_half(g, (2,))

    lane_q = lax.broadcasted_iota(jnp.int32, (32, 128), 1)
    for at, raw in enumerate((w1, w2)):
        for q in range(32):
            spread[32 * q:32 * q + 27, :] = raw[:, 128 * q:128 * q + 128].astype(F32)

        def tap_rows(e):
            return spread[pl.ds(e, 32, stride=32), :]

        for kw in range(3):
            for m in range(5):
                here = tap_rows(6 * m + kw)
                after = tap_rows(6 * m + 3 + kw) if m < 4 else jnp.zeros((32, 128), F32)
                packed[m, pl.ds(64 * kw, 32, stride=2), :] = jnp.where(
                    lane_q < 64, here, pltpu.roll(after, 64, 1))
                packed[m, pl.ds(64 * kw + 1, 32, stride=2), :] = jnp.where(
                    lane_q < 64, pltpu.roll(here, 64, 1), after)
        for m in range(5):
            wconv[at, :, 128 * m:128 * m + 128] = packed[m].astype(BF)

    def forward(half):
        @pl.when(exists(d - s))
        def _():
            arrived(2 - s, half)
            to_depth(half, 3, 2 - s, d + s).start()

    forward(f)
    w_other = pl.ds(8 * (1 - core), 8)
    w_copy.wait_recv()
    w_forward = pltpu.make_async_remote_copy(
        src_ref=wup.at[w_half, g], dst_ref=wup.at[w_half, g], send_sem=wsend.at[1], recv_sem=wrecv.at[1],
        device_id=(d + s, f), device_id_type=MESH)
    w_forward.start()
    forward(g)
    for half in range(2):
        arrived(2 + s, half)
    w_forward.wait_recv()

    lane = lax.broadcasted_iota(jnp.int32, (64, 128), 1)
    lane_in = lax.broadcasted_iota(jnp.int32, (128, 128), 1)
    row_at = lax.broadcasted_iota(jnp.int32, (256, 256), 0)
    col_at = lax.broadcasted_iota(jnp.int32, (256, 256), 1)
    odd, rest = row_at // 128, row_at % 128
    place = jnp.where(col_at == 128 * (rest // 64) + 2 * (rest % 64) + odd, 1.0, 0.0).astype(BF)

    def column(row, count):
        at = lax.broadcasted_iota(jnp.int32, (count, count), 0)
        to = lax.broadcasted_iota(jnp.int32, (count, count), 1)
        return jnp.sum(jnp.where(at == to, row, 0.0), axis=1, keepdims=True)

    b_copy.wait_recv()
    mine, other = column(bmine[0:1, 0:32], 32), column(bother[0:1, 0:32], 32)
    bias_up = jnp.concatenate([jnp.where(f == 0, mine, other), jnp.where(f == 0, other, mine)], axis=0)
    bias_1, bias_2 = column(b1[...], 64), column(b2[...], 64)

    def shifted(slot):
        whole = grid_in[slot].reshape(128, 640).astype(F32)
        zero = jnp.zeros((128, 128), F32)
        turned = [zero] + [pltpu.roll(whole[:, 128 * t:128 * t + 128], 64, 1) for t in range(5)] + [zero]
        for t in range(6):
            moved[slot, :, 128 * t:128 * t + 128] = jnp.where(lane_in < 64, turned[t], turned[t + 1]).astype(BF)

    def upsample_plane(p):
        q, pd = p // 2, p % 2
        inside = exists(d - 1 + q)
        slots = (q + 1, q + 2 * pd)
        kds = (1 + pd, 3 - 3 * pd)
        for ph in range(2):
            khs = (1 + ph, 3 - 3 * ph)
            left, right = [], []
            for slot, kd in zip(slots, kds):
                for at, kh in enumerate(khs):
                    left.append(wup[4 * kd + kh].reshape(256, 128))
                    if at == 0:
                        right.append(grid_in[slot].reshape(128, 640))
                    else:
                        right.append(moved[slot, :, 128 * ph:128 * ph + 640])
            total = jnp.dot(jnp.concatenate(left, axis=1), jnp.concatenate(right, axis=0),
                            preferred_element_type=F32)
            rows = []
            for t in range(5):
                cols = slice(128 * t, 128 * t + 128)
                tap = [jnp.concatenate([total[32 * k:32 * k + 32, cols], total[128 + 32 * k:160 + 32 * k, cols]], axis=0)
                       for k in range(4)]
                even = tap[1] + jnp.where(lane % 64 > 0, pltpu.roll(tap[3], 1, 1), 0.0) + bias_up
                odd_ = tap[2] + jnp.where(lane % 64 < 63, pltpu.roll(tap[0], 127, 1), 0.0) + bias_up
                rows.append(jnp.concatenate([even, odd_], axis=1))
            both = jnp.where(inside, jnp.concatenate(rows, axis=0), 0.0).astype(BF)
            mixed = jnp.dot(both, place, preferred_element_type=F32).astype(BF)
            for t in range(5):
                for r in range(2):
                    ups[p, 1 + 2 * (2 * t + r) + ph] = mixed[64 * t:64 * t + 64, 128 * r:128 * r + 128]

    for slot in (1, 2, 3):
        shifted(slot)
    lax.fori_loop(1, 5, lambda p, c: (upsample_plane(p), c)[1], 0)

    first, second = wconv[0, :, 0:576], wconv[1, :, 0:576]

    def hidden_step(i, c):
        plane, row = i // 3, 6 * (i % 3)
        at = 2 * d - 1 + plane
        inside = jnp.logical_and(at >= 0, at < 2 * devices)
        for r, value in enumerate(conv_rows(ups, first, bias_1, plane, 2 * f + row, 6, lane)):
            hid[plane, 1 + row + r] = jnp.where(inside, value, 0.0).astype(BF)
        return c

    lax.fori_loop(3, 9, hidden_step, 0)

    for half in range(2):
        @pl.when(exists(d - 2 * s))
        def _():
            arrived(2 - 2 * s, half)

        @pl.when(exists(d + 2 * s))
        def _():
            arrived(2 + 2 * s, half)
    for slot in (0, 4):
        shifted(slot)
    lax.fori_loop(0, 2, lambda i, c: (upsample_plane(5 * i), c)[1], 0)
    lax.fori_loop(0, 6, lambda i, c: hidden_step(i + 6 * (i // 3), c), 0)

    rows_mine = pl.ds(16 * f, 16)

    def out_copy(plane):
        return pltpu.make_async_remote_copy(
            src_ref=result.at[plane, g], dst_ref=out.at[plane, rows_mine],
            send_sem=osend.at[plane], recv_sem=orecv.at[plane], device_id=(d, g), device_id_type=MESH)

    def own_copy(plane):
        return pltpu.make_async_copy(result.at[plane, f], out.at[plane, rows_mine], lsem.at[plane])

    for plane in range(2):
        def step(i, c):
            row = 4 * i
            for r, value in enumerate(conv_rows(hid, second, bias_2, plane, 2 * f + row, 4, lane)):
                value = value.astype(BF)
                result[plane, 0, row + r] = value[0:32]
                result[plane, 1, row + r] = value[32:64]
            return c

        lax.fori_loop(0, 4, step, 0)
        out_copy(plane).start()
        own_copy(plane).start()

    b_copy.wait_send()
    x_copy.wait_send()
    w_copy.wait_send()
    w_forward.wait_send()
    for half in range(2):
        for which, off in enumerate((-s, s, 2 * s)):
            @pl.when(exists(d + off))
            def _():
                to_depth(half, which, 2, d + off).wait_send()

        @pl.when(exists(d - s))
        def _():
            to_depth(half, 3, 2 - s, d + s).wait_send()
    for plane in range(2):
        own_copy(plane).wait()
        out_copy(plane).wait()


def shards(devices, volume, up_weight, up_bias, first_weight, first_bias, second_weight, second_bias):
    vol = volume.reshape(64, 1024)
    wt = jnp.transpose(up_weight.reshape(128, 32, 16, 4), (2, 3, 1, 0)).reshape(16, 128, 128)
    vmem = pl.BlockSpec(memory_space=pltpu.VMEM)
    out = pl.pallas_call(
        functools.partial(kernel, devices),
        out_shape=jax.ShapeDtypeStruct((2, 32, 32, 128), BF),
        in_specs=[vmem] * 7,
        out_specs=vmem,
        scratch_shapes=[
            pltpu.VMEM((5, 2, 64, 640), BF),
            pltpu.VMEM((5, 128, 768), BF),
            pltpu.VMEM((16, 2, 128, 128), BF),
            pltpu.VMEM((6, 22, 64, 128), BF),
            pltpu.VMEM((4, 20, 64, 128), BF),
            pltpu.VMEM((2, 2, 16, 32, 128), BF),
            pltpu.VMEM((8, 128), F32),
            pltpu.VMEM((8, 128), F32),
            pltpu.VMEM((1024, 128), F32),
            pltpu.VMEM((5, 192, 128), F32),
            pltpu.VMEM((2, 192, 640), BF),
            pltpu.SemaphoreType.DMA((4, 2)),
            pltpu.SemaphoreType.DMA((5, 2)),
            pltpu.SemaphoreType.DMA,
            pltpu.SemaphoreType.DMA((2,)),
            pltpu.SemaphoreType.DMA((2,)),
            pltpu.SemaphoreType.DMA((2,)),
            pltpu.SemaphoreType.DMA((2,)),
            pltpu.SemaphoreType.DMA((2,)),
            pltpu.SemaphoreType.DMA((2,)),
        ],
        compiler_params=pltpu.CompilerParams(
            collective_id=0, has_side_effects=True, vmem_limit_bytes=48 * 1024 * 1024),
    )(vol, wt, first_weight, second_weight, up_bias[None], first_bias[None], second_bias[None])
    return jnp.transpose(out, (2, 0, 1, 3))


def solution(mesh):
    placed = (P("filt", "depth", None), P(None, "filt"), P("filt"), P(), P(), P(), P())
    return jax.shard_map(
        functools.partial(shards, mesh.shape["depth"]),
        mesh=mesh,
        in_specs=placed,
        out_specs=P("filt", "depth", None, None),
        check_vma=False,
    )
```

```python
import functools

import jax
import jax.numpy as jnp
from jax import lax
from jax.experimental import pallas as pl
from jax.experimental.pallas import tpu as pltpu
from jax.sharding import PartitionSpec as P

BF = jnp.bfloat16
F32 = jnp.float32
MESH = pl.DeviceIdType.MESH


def shift_add(low, mid, high, lane):
    left = jnp.where(lane > 0, pltpu.roll(low, 1, 1), 0.0)
    right = jnp.where(lane < 127, pltpu.roll(high, 127, 1), 0.0)
    return mid + left + right


def conv_rows(src, weight, bias, places, lane):
    groups = []
    for plane, row in places:
        groups.append(jnp.concatenate([src[plane + kd, row + i] for kd in range(3) for i in range(4)], axis=0))
    total = jnp.dot(weight, jnp.concatenate(groups, axis=1), preferred_element_type=F32)
    outs = []
    for at in range(len(places)):
        cols = slice(128 * at, 128 * at + 128)
        for j in range(2):
            base = 192 * j
            value = shift_add(total[base:base + 64, cols], total[base + 64:base + 128, cols],
                              total[base + 128:base + 192, cols], lane)
            value = value + bias
            outs.append(jnp.maximum(value, 0.2 * value))
    return outs


def kernel(devices, vol, wt, w1, w2, bu, b1, b2, out,
           grid_in, moved, wup, ups, hid, result, bmine, bother, spread, packed, wconv,
           send, recv, xsend, wsend, wrecv, osend, orecv, lsem, bsem):
    d = lax.axis_index("depth")
    f = lax.axis_index("filt")
    g = 1 - f
    core = lax.rem(d, 2)
    s = 1 - 2 * core

    def exists(t):
        return jnp.logical_and(t >= 0, t < devices)

    barrier = pltpu.get_barrier_semaphore()
    pl.semaphore_signal(barrier, inc=1, device_id=(d, g), device_id_type=MESH)
    for off in (-2, -1, 1, 2):
        @pl.when(exists(d + off))
        def _():
            pl.semaphore_signal(barrier, inc=1, device_id=(d + off, f), device_id_type=MESH)
    peers = 1
    for off in (-2, -1, 1, 2):
        peers = peers + jnp.where(exists(d + off), 1, 0)
    pl.semaphore_wait(barrier, peers)

    x_copy = pltpu.make_async_remote_copy(
        src_ref=vol.at[:, pl.ds(pl.multiple_of(384 * g, 128), 640)],
        dst_ref=grid_in.at[2, f], send_sem=xsend, recv_sem=recv.at[2, f],
        device_id=(d, g), device_id_type=MESH)
    x_copy.start()
    w_half = pl.ds(8 * core, 8)
    w_copy = pltpu.make_async_remote_copy(
        src_ref=wt.at[w_half], dst_ref=wup.at[w_half, f], send_sem=wsend.at[0], recv_sem=wrecv.at[0],
        device_id=(d, g), device_id_type=MESH)
    w_copy.start()
    bmine[...] = jnp.zeros((8, 128), F32)
    bmine[0:1, 0:32] = bu[...]
    b_copy = pltpu.make_async_remote_copy(
        src_ref=bmine, dst_ref=bother, send_sem=bsem.at[0], recv_sem=bsem.at[1],
        device_id=(d, g), device_id_type=MESH)
    b_copy.start()
    grid_in[2, f] = vol[:, pl.ds(pl.multiple_of(384 * f, 128), 640)]

    def to_depth(half, which, at, target):
        slot = d - target + 2 if which < 3 else 2 - 2 * s
        return pltpu.make_async_remote_copy(
            src_ref=grid_in.at[at, half], dst_ref=grid_in.at[slot, half],
            send_sem=send.at[which, half], recv_sem=recv.at[slot, half],
            device_id=(target, f), device_id_type=MESH)

    def arrived(slot, half):
        pltpu.make_async_copy(grid_in.at[slot, half], grid_in.at[slot, half], recv.at[slot, half]).wait()

    def start_half(half, some):
        for which in some:
            off = (-s, s, 2 * s)[which]

            @pl.when(exists(d + off))
            def _():
                to_depth(half, which, 2, d + off).start()

    start_half(f, (0, 1))
    for off in (-2, -1, 1, 2):
        @pl.when(jnp.logical_not(exists(d + off)))
        def _():
            grid_in[2 + off] = jnp.zeros(grid_in.shape[1:], BF)
    for k in range(16):
        wup[k, f] = wt[k]
    ups[:, 0] = jnp.zeros((6, 64, 128), BF)
    ups[:, 21] = jnp.zeros((6, 64, 128), BF)
    hid[:, 0] = jnp.zeros((4, 64, 128), BF)
    hid[:, 19] = jnp.zeros((4, 64, 128), BF)

    x_recv = pltpu.make_async_copy(grid_in.at[2, g], grid_in.at[2, g], recv.at[2, g])
    x_recv.wait()
    start_half(g, (0, 1))
    start_half(f, (2,))
    start_half(g, (2,))

    lane_q = lax.broadcasted_iota(jnp.int32, (32, 128), 1)
    for at, raw in enumerate((w1, w2)):
        for q in range(32):
            spread[32 * q:32 * q + 27, :] = raw[:, 128 * q:128 * q + 128].astype(F32)

        def tap_rows(e):
            return spread[pl.ds(e, 32, stride=32), :]

        nothing = jnp.zeros((32, 128), F32)
        for kw in range(3):
            for kd in range(3):
                rows_of = [tap_rows(9 * kd + 3 * kh + kw) for kh in range(3)]
                turned = [pltpu.roll(value, 64, 1) for value in rows_of]
                for j in range(2):
                    for pair in range(2):
                        m, base = 2 * kd + pair, 192 * j + 64 * kw
                        low, high = 2 * pair - j, 2 * pair + 1 - j
                        even = rows_of[low] if 0 <= low < 3 else nothing
                        odd_ = turned[high] if 0 <= high < 3 else nothing
                        packed[m, pl.ds(base, 32, stride=2), :] = jnp.where(lane_q < 64, even, odd_)
                        even = turned[low] if 0 <= low < 3 else nothing
                        odd_ = rows_of[high] if 0 <= high < 3 else nothing
                        packed[m, pl.ds(base + 1, 32, stride=2), :] = jnp.where(lane_q < 64, even, odd_)
        for m in range(6):
            wconv[at, :, 128 * m:128 * m + 128] = packed[m].astype(BF)

    def forward(half):
        @pl.when(exists(d - s))
        def _():
            arrived(2 - s, half)
            to_depth(half, 3, 2 - s, d + s).start()

    forward(f)
    w_other = pl.ds(8 * (1 - core), 8)
    w_copy.wait_recv()
    w_forward = pltpu.make_async_remote_copy(
        src_ref=wup.at[w_half, g], dst_ref=wup.at[w_half, g], send_sem=wsend.at[1], recv_sem=wrecv.at[1],
        device_id=(d + s, f), device_id_type=MESH)
    w_forward.start()
    forward(g)
    for half in range(2):
        arrived(2 + s, half)
    w_forward.wait_recv()

    lane = lax.broadcasted_iota(jnp.int32, (64, 128), 1)
    lane_in = lax.broadcasted_iota(jnp.int32, (128, 128), 1)
    row_at = lax.broadcasted_iota(jnp.int32, (256, 256), 0)
    col_at = lax.broadcasted_iota(jnp.int32, (256, 256), 1)
    odd, rest = row_at // 128, row_at % 128
    place = jnp.where(col_at == 128 * (rest // 64) + 2 * (rest % 64) + odd, 1.0, 0.0).astype(BF)

    def column(row, count):
        at = lax.broadcasted_iota(jnp.int32, (count, count), 0)
        to = lax.broadcasted_iota(jnp.int32, (count, count), 1)
        return jnp.sum(jnp.where(at == to, row, 0.0), axis=1, keepdims=True)

    b_copy.wait_recv()
    mine, other = column(bmine[0:1, 0:32], 32), column(bother[0:1, 0:32], 32)
    bias_up = jnp.concatenate([jnp.where(f == 0, mine, other), jnp.where(f == 0, other, mine)], axis=0)
    bias_1, bias_2 = column(b1[...], 64), column(b2[...], 64)

    def shifted(slot):
        whole = grid_in[slot].reshape(128, 640).astype(F32)
        zero = jnp.zeros((128, 128), F32)
        turned = [zero] + [pltpu.roll(whole[:, 128 * t:128 * t + 128], 64, 1) for t in range(5)] + [zero]
        for t in range(6):
            moved[slot, :, 128 * t:128 * t + 128] = jnp.where(lane_in < 64, turned[t], turned[t + 1]).astype(BF)

    def upsample_plane(p):
        q, pd = p // 2, p % 2
        inside = exists(d - 1 + q)
        slots = (q + 1, q + 2 * pd)
        kds = (1 + pd, 3 - 3 * pd)
        for ph in range(2):
            khs = (1 + ph, 3 - 3 * ph)
            left, right = [], []
            for slot, kd in zip(slots, kds):
                for at, kh in enumerate(khs):
                    left.append(wup[4 * kd + kh].reshape(256, 128))
                    if at == 0:
                        right.append(grid_in[slot].reshape(128, 640))
                    else:
                        right.append(moved[slot, :, 128 * ph:128 * ph + 640])
            total = jnp.dot(jnp.concatenate(left, axis=1), jnp.concatenate(right, axis=0),
                            preferred_element_type=F32)
            rows = []
            for t in range(5):
                cols = slice(128 * t, 128 * t + 128)
                tap = [jnp.concatenate([total[32 * k:32 * k + 32, cols], total[128 + 32 * k:160 + 32 * k, cols]], axis=0)
                       for k in range(4)]
                even = tap[1] + jnp.where(lane % 64 > 0, pltpu.roll(tap[3], 1, 1), 0.0) + bias_up
                odd_ = tap[2] + jnp.where(lane % 64 < 63, pltpu.roll(tap[0], 127, 1), 0.0) + bias_up
                rows.append(jnp.concatenate([even, odd_], axis=1))
            both = jnp.where(inside, jnp.concatenate(rows, axis=0), 0.0).astype(BF)
            mixed = jnp.dot(both, place, preferred_element_type=F32).astype(BF)
            for t in range(5):
                for r in range(2):
                    ups[p, 1 + 2 * (2 * t + r) + ph] = mixed[64 * t:64 * t + 64, 128 * r:128 * r + 128]

    for slot in (1, 2, 3):
        shifted(slot)
    lax.fori_loop(1, 5, lambda p, c: (upsample_plane(p), c)[1], 0)

    def hidden_pass(planes):
        def step(i, c):
            places, spots = [], []
            for r in range(6):
                group = 6 * i + r
                plane = planes[0] + (planes[1] - planes[0]) * (group // 9)
                row = 2 * (group % 9)
                places.append((plane, 2 * f + row))
                spots.append((plane, row))
            values = conv_rows(ups, wconv[0], bias_1, places, lane)
            for r, (plane, row) in enumerate(spots):
                at = 2 * d - 1 + plane
                inside = jnp.logical_and(at >= 0, at < 2 * devices)
                for j in range(2):
                    hid[plane, 1 + row + j] = jnp.where(inside, values[2 * r + j], 0.0).astype(BF)
            return c

        lax.fori_loop(0, 3, step, 0)

    hidden_pass((1, 2))

    for half in range(2):
        @pl.when(exists(d - 2 * s))
        def _():
            arrived(2 - 2 * s, half)

        @pl.when(exists(d + 2 * s))
        def _():
            arrived(2 + 2 * s, half)
    for slot in (0, 4):
        shifted(slot)
    lax.fori_loop(0, 2, lambda i, c: (upsample_plane(5 * i), c)[1], 0)
    hidden_pass((0, 3))

    rows_mine = pl.ds(16 * f, 16)

    def out_copy(plane):
        return pltpu.make_async_remote_copy(
            src_ref=result.at[plane, g], dst_ref=out.at[plane, rows_mine],
            send_sem=osend.at[plane], recv_sem=orecv.at[plane], device_id=(d, g), device_id_type=MESH)

    def own_copy(plane):
        return pltpu.make_async_copy(result.at[plane, f], out.at[plane, rows_mine], lsem.at[plane])

    for plane in range(2):
        def step(i, c):
            row = 8 * i
            places = [(plane, 2 * f + row + 2 * r) for r in range(4)]
            for r, value in enumerate(conv_rows(hid, wconv[1], bias_2, places, lane)):
                value = value.astype(BF)
                result[plane, 0, row + r] = value[0:32]
                result[plane, 1, row + r] = value[32:64]
            return c

        lax.fori_loop(0, 2, step, 0)
        out_copy(plane).start()
        own_copy(plane).start()

    b_copy.wait_send()
    x_copy.wait_send()
    w_copy.wait_send()
    w_forward.wait_send()
    for half in range(2):
        for which, off in enumerate((-s, s, 2 * s)):
            @pl.when(exists(d + off))
            def _():
                to_depth(half, which, 2, d + off).wait_send()

        @pl.when(exists(d - s))
        def _():
            to_depth(half, 3, 2 - s, d + s).wait_send()
    for plane in range(2):
        own_copy(plane).wait()
        out_copy(plane).wait()


def shards(devices, volume, up_weight, up_bias, first_weight, first_bias, second_weight, second_bias):
    vol = volume.reshape(64, 1024)
    wt = jnp.transpose(up_weight.reshape(128, 32, 16, 4), (2, 3, 1, 0)).reshape(16, 128, 128)
    vmem = pl.BlockSpec(memory_space=pltpu.VMEM)
    out = pl.pallas_call(
        functools.partial(kernel, devices),
        out_shape=jax.ShapeDtypeStruct((2, 32, 32, 128), BF),
        in_specs=[vmem] * 7,
        out_specs=vmem,
        scratch_shapes=[
            pltpu.VMEM((5, 2, 64, 640), BF),
            pltpu.VMEM((5, 128, 768), BF),
            pltpu.VMEM((16, 2, 128, 128), BF),
            pltpu.VMEM((6, 22, 64, 128), BF),
            pltpu.VMEM((4, 20, 64, 128), BF),
            pltpu.VMEM((2, 2, 16, 32, 128), BF),
            pltpu.VMEM((8, 128), F32),
            pltpu.VMEM((8, 128), F32),
            pltpu.VMEM((1024, 128), F32),
            pltpu.VMEM((6, 384, 128), F32),
            pltpu.VMEM((2, 384, 768), BF),
            pltpu.SemaphoreType.DMA((4, 2)),
            pltpu.SemaphoreType.DMA((5, 2)),
            pltpu.SemaphoreType.DMA,
            pltpu.SemaphoreType.DMA((2,)),
            pltpu.SemaphoreType.DMA((2,)),
            pltpu.SemaphoreType.DMA((2,)),
            pltpu.SemaphoreType.DMA((2,)),
            pltpu.SemaphoreType.DMA((2,)),
            pltpu.SemaphoreType.DMA((2,)),
        ],
        compiler_params=pltpu.CompilerParams(
            collective_id=0, has_side_effects=True, vmem_limit_bytes=48 * 1024 * 1024),
    )(vol, wt, first_weight, second_weight, up_bias[None], first_bias[None], second_bias[None])
    return jnp.transpose(out, (2, 0, 1, 3))


def solution(mesh):
    placed = (P("filt", "depth", None), P(None, "filt"), P("filt"), P(), P(), P(), P())
    return jax.shard_map(
        functools.partial(shards, mesh.shape["depth"]),
        mesh=mesh,
        in_specs=placed,
        out_specs=P("filt", "depth", None, None),
        check_vma=False,
    )
```

```python
import functools

import jax
import jax.numpy as jnp
from jax import lax
from jax.experimental import pallas as pl
from jax.experimental.pallas import tpu as pltpu
from jax.sharding import PartitionSpec as P

BF = jnp.bfloat16
F32 = jnp.float32
MESH = pl.DeviceIdType.MESH


def shift_add(low, mid, high, lane):
    left = jnp.where(lane > 0, pltpu.roll(low, 1, 1), 0.0)
    right = jnp.where(lane < 127, pltpu.roll(high, 127, 1), 0.0)
    return mid + left + right


def conv_rows(src, weight, bias, places, lane):
    groups = []
    for plane, row in places:
        groups.append(jnp.concatenate([src[plane + kd, row + i] for kd in range(3) for i in range(4)], axis=0))
    total = jnp.dot(weight, jnp.concatenate(groups, axis=1), preferred_element_type=F32)
    outs = []
    for at in range(len(places)):
        cols = slice(128 * at, 128 * at + 128)
        for j in range(2):
            base = 192 * j
            value = shift_add(total[base:base + 64, cols], total[base + 64:base + 128, cols],
                              total[base + 128:base + 192, cols], lane)
            value = value + bias
            outs.append(jnp.maximum(value, 0.2 * value))
    return outs


def kernel(devices, vol, wt, w1, w2, bu, b1, b2, out,
           grid_in, moved, wup, ups, hid, result, bmine, bother, spread, packed, wconv,
           send, recv, xsend, wsend, wrecv, osend, orecv, lsem, bsem):
    d = lax.axis_index("depth")
    f = lax.axis_index("filt")
    g = 1 - f
    core = lax.rem(d, 2)
    s = 1 - 2 * core

    def exists(t):
        return jnp.logical_and(t >= 0, t < devices)

    barrier = pltpu.get_barrier_semaphore()
    pl.semaphore_signal(barrier, inc=1, device_id=(d, g), device_id_type=MESH)
    for off in (-2, -1, 1, 2):
        @pl.when(exists(d + off))
        def _():
            pl.semaphore_signal(barrier, inc=1, device_id=(d + off, f), device_id_type=MESH)
    peers = 1
    for off in (-2, -1, 1, 2):
        peers = peers + jnp.where(exists(d + off), 1, 0)
    pl.semaphore_wait(barrier, peers)

    x_copy = pltpu.make_async_remote_copy(
        src_ref=vol.at[:, pl.ds(pl.multiple_of(384 * g, 128), 640)],
        dst_ref=grid_in.at[2, f], send_sem=xsend, recv_sem=recv.at[2, f],
        device_id=(d, g), device_id_type=MESH)
    x_copy.start()
    w_half = pl.ds(8 * core, 8)
    w_copy = pltpu.make_async_remote_copy(
        src_ref=wt.at[w_half], dst_ref=wup.at[w_half, f], send_sem=wsend.at[0], recv_sem=wrecv.at[0],
        device_id=(d, g), device_id_type=MESH)
    w_copy.start()
    bmine[...] = jnp.zeros((8, 128), F32)
    bmine[0:1, 0:32] = bu[...]
    b_copy = pltpu.make_async_remote_copy(
        src_ref=bmine, dst_ref=bother, send_sem=bsem.at[0], recv_sem=bsem.at[1],
        device_id=(d, g), device_id_type=MESH)
    b_copy.start()
    grid_in[2, f] = vol[:, pl.ds(pl.multiple_of(384 * f, 128), 640)]

    def to_depth(half, which, at, target):
        slot = d - target + 2 if which < 3 else 2 - 2 * s
        return pltpu.make_async_remote_copy(
            src_ref=grid_in.at[at, half], dst_ref=grid_in.at[slot, half],
            send_sem=send.at[which, half], recv_sem=recv.at[slot, half],
            device_id=(target, f), device_id_type=MESH)

    def arrived(slot, half):
        pltpu.make_async_copy(grid_in.at[slot, half], grid_in.at[slot, half], recv.at[slot, half]).wait()

    def start_half(half, some):
        for which in some:
            off = (-s, s, 2 * s)[which]

            @pl.when(exists(d + off))
            def _():
                to_depth(half, which, 2, d + off).start()

    start_half(f, (0, 1))
    for off in (-2, -1, 1, 2):
        @pl.when(jnp.logical_not(exists(d + off)))
        def _():
            grid_in[2 + off] = jnp.zeros(grid_in.shape[1:], BF)
    for k in range(16):
        wup[k, f] = wt[k]
    ups[:, 0] = jnp.zeros((6, 64, 128), BF)
    ups[:, 21] = jnp.zeros((6, 64, 128), BF)
    hid[:, 0] = jnp.zeros((4, 64, 128), BF)
    hid[:, 19] = jnp.zeros((4, 64, 128), BF)

    lane_q = lax.broadcasted_iota(jnp.int32, (32, 128), 1)
    def rearrange(at, raw):
        for q in range(32):
            spread[32 * q:32 * q + 27, :] = raw[:, 128 * q:128 * q + 128].astype(F32)

        def tap_rows(e):
            return spread[pl.ds(e, 32, stride=32), :]

        nothing = jnp.zeros((32, 128), F32)
        for kw in range(3):
            for kd in range(3):
                rows_of = [tap_rows(9 * kd + 3 * kh + kw) for kh in range(3)]
                turned = [pltpu.roll(value, 64, 1) for value in rows_of]
                for j in range(2):
                    for pair in range(2):
                        m, base = 2 * kd + pair, 192 * j + 64 * kw
                        low, high = 2 * pair - j, 2 * pair + 1 - j
                        even = rows_of[low] if 0 <= low < 3 else nothing
                        odd_ = turned[high] if 0 <= high < 3 else nothing
                        packed[m, pl.ds(base, 32, stride=2), :] = jnp.where(lane_q < 64, even, odd_)
                        even = turned[low] if 0 <= low < 3 else nothing
                        odd_ = rows_of[high] if 0 <= high < 3 else nothing
                        packed[m, pl.ds(base + 1, 32, stride=2), :] = jnp.where(lane_q < 64, even, odd_)
        for m in range(6):
            wconv[at, :, 128 * m:128 * m + 128] = packed[m].astype(BF)

    rearrange(0, w1)

    x_recv = pltpu.make_async_copy(grid_in.at[2, g], grid_in.at[2, g], recv.at[2, g])
    x_recv.wait()
    start_half(g, (0, 1))
    start_half(f, (2,))
    start_half(g, (2,))

    rearrange(1, w2)

    def forward(half):
        @pl.when(exists(d - s))
        def _():
            arrived(2 - s, half)
            to_depth(half, 3, 2 - s, d + s).start()

    forward(f)
    forward(g)
    for half in range(2):
        arrived(2 + s, half)
    w_forward = pltpu.make_async_remote_copy(
        src_ref=wup.at[w_half, g], dst_ref=wup.at[w_half, g], send_sem=wsend.at[1], recv_sem=wrecv.at[1],
        device_id=(d + s, f), device_id_type=MESH)

    lane = lax.broadcasted_iota(jnp.int32, (64, 128), 1)
    lane_in = lax.broadcasted_iota(jnp.int32, (128, 128), 1)
    row_at = lax.broadcasted_iota(jnp.int32, (256, 256), 0)
    col_at = lax.broadcasted_iota(jnp.int32, (256, 256), 1)
    odd, rest = row_at // 128, row_at % 128
    place = jnp.where(col_at == 128 * (rest // 64) + 2 * (rest % 64) + odd, 1.0, 0.0).astype(BF)

    def column(row, count):
        at = lax.broadcasted_iota(jnp.int32, (count, count), 0)
        to = lax.broadcasted_iota(jnp.int32, (count, count), 1)
        return jnp.sum(jnp.where(at == to, row, 0.0), axis=1, keepdims=True)

    b_copy.wait_recv()
    mine, other = column(bmine[0:1, 0:32], 32), column(bother[0:1, 0:32], 32)
    bias_1, bias_2 = column(b1[...], 64), column(b2[...], 64)

    def shifted(slot):
        whole = grid_in[slot].reshape(128, 640).astype(F32)
        zero = jnp.zeros((128, 128), F32)
        turned = [zero] + [pltpu.roll(whole[:, 128 * t:128 * t + 128], 64, 1) for t in range(5)] + [zero]
        for t in range(6):
            moved[slot, :, 128 * t:128 * t + 128] = jnp.where(lane_in < 64, turned[t], turned[t + 1]).astype(BF)

    lane_half = lax.broadcasted_iota(jnp.int32, (32, 128), 1) % 64

    def upsample_plane(p, half, bias_up):
        rows_at = pl.ds(pl.multiple_of(32 * half, 32), 32)
        q, pd = p // 2, p % 2
        inside = exists(d - 1 + q)
        slots = (q + 1, q + 2 * pd)
        kds = (1 + pd, 3 - 3 * pd)
        for ph in range(2):
            khs = (1 + ph, 3 - 3 * ph)
            left, right = [], []
            for slot, kd in zip(slots, kds):
                for at, kh in enumerate(khs):
                    left.append(wup[4 * kd + kh, half])
                    if at == 0:
                        right.append(grid_in[slot].reshape(128, 640))
                    else:
                        right.append(moved[slot, :, 128 * ph:128 * ph + 640])
            total = jnp.dot(jnp.concatenate(left, axis=1), jnp.concatenate(right, axis=0),
                            preferred_element_type=F32)
            rows = []
            for t in range(5):
                cols = slice(128 * t, 128 * t + 128)
                tap = [total[32 * k:32 * k + 32, cols] for k in range(4)]
                even = tap[1] + jnp.where(lane_half > 0, pltpu.roll(tap[3], 1, 1), 0.0) + bias_up
                odd_ = tap[2] + jnp.where(lane_half < 63, pltpu.roll(tap[0], 127, 1), 0.0) + bias_up
                rows.append(jnp.concatenate([even, odd_], axis=1))
            both = jnp.where(inside, jnp.concatenate(rows, axis=0), 0.0).astype(BF)
            mixed = jnp.dot(both, place, preferred_element_type=F32).astype(BF)
            for t in range(5):
                for r in range(2):
                    ups[p, 1 + 2 * (2 * t + r) + ph, rows_at, :] = mixed[32 * t:32 * t + 32, 128 * r:128 * r + 128]

    for slot in (1, 2, 3):
        shifted(slot)

    def upsample_own(p, c):
        upsample_plane(p, f, mine)
        return c

    def upsample_other(p, c):
        upsample_plane(p, g, other)
        return c

    lax.fori_loop(1, 3, upsample_own, 0)
    w_copy.wait_recv()
    w_forward.start()
    lax.fori_loop(3, 5, upsample_own, 0)
    w_forward.wait_recv()
    lax.fori_loop(1, 5, upsample_other, 0)

    def hidden_pass(planes):
        def step(i, c):
            places, spots = [], []
            for r in range(6):
                group = 6 * i + r
                plane = planes[0] + (planes[1] - planes[0]) * (group // 9)
                row = 2 * (group % 9)
                places.append((plane, 2 * f + row))
                spots.append((plane, row))
            values = conv_rows(ups, wconv[0], bias_1, places, lane)
            for r, (plane, row) in enumerate(spots):
                at = 2 * d - 1 + plane
                inside = jnp.logical_and(at >= 0, at < 2 * devices)
                for j in range(2):
                    hid[plane, 1 + row + j] = jnp.where(inside, values[2 * r + j], 0.0).astype(BF)
            return c

        lax.fori_loop(0, 3, step, 0)

    hidden_pass((1, 2))

    for half in range(2):
        @pl.when(exists(d - 2 * s))
        def _():
            arrived(2 - 2 * s, half)

        @pl.when(exists(d + 2 * s))
        def _():
            arrived(2 + 2 * s, half)
    for slot in (0, 4):
        shifted(slot)
    lax.fori_loop(0, 2, lambda i, c: upsample_other(5 * i, upsample_own(5 * i, c)), 0)
    hidden_pass((0, 3))

    def piece(k):
        return result.at[k // 2, :, pl.ds(8 * (k % 2), 8)], out.at[k // 2, pl.ds(16 * f + 8 * (k % 2), 8)]

    def out_copy(k):
        source, target = piece(k)
        return pltpu.make_async_remote_copy(
            src_ref=source.at[g], dst_ref=target,
            send_sem=osend.at[k], recv_sem=orecv.at[k], device_id=(d, g), device_id_type=MESH)

    def own_copy(k):
        source, target = piece(k)
        return pltpu.make_async_copy(source.at[f], target, lsem.at[k])

    for k in range(4):
        plane, row = k // 2, 8 * (k % 2)
        places = [(plane, 2 * f + row + 2 * r) for r in range(4)]
        for r, value in enumerate(conv_rows(hid, wconv[1], bias_2, places, lane)):
            value = value.astype(BF)
            result[plane, 0, row + r] = value[0:32]
            result[plane, 1, row + r] = value[32:64]
        out_copy(k).start()
        own_copy(k).start()

    b_copy.wait_send()
    x_copy.wait_send()
    w_copy.wait_send()
    w_forward.wait_send()
    for half in range(2):
        for which, off in enumerate((-s, s, 2 * s)):
            @pl.when(exists(d + off))
            def _():
                to_depth(half, which, 2, d + off).wait_send()

        @pl.when(exists(d - s))
        def _():
            to_depth(half, 3, 2 - s, d + s).wait_send()
    for k in range(4):
        own_copy(k).wait()
        out_copy(k).wait()


def shards(devices, volume, up_weight, up_bias, first_weight, first_bias, second_weight, second_bias):
    vol = volume.reshape(64, 1024)
    wt = jnp.transpose(up_weight.reshape(128, 32, 16, 4), (2, 3, 1, 0)).reshape(16, 128, 128)
    vmem = pl.BlockSpec(memory_space=pltpu.VMEM)
    out = pl.pallas_call(
        functools.partial(kernel, devices),
        out_shape=jax.ShapeDtypeStruct((2, 32, 32, 128), BF),
        in_specs=[vmem] * 7,
        out_specs=vmem,
        scratch_shapes=[
            pltpu.VMEM((5, 2, 64, 640), BF),
            pltpu.VMEM((5, 128, 768), BF),
            pltpu.VMEM((16, 2, 128, 128), BF),
            pltpu.VMEM((6, 22, 64, 128), BF),
            pltpu.VMEM((4, 20, 64, 128), BF),
            pltpu.VMEM((2, 2, 16, 32, 128), BF),
            pltpu.VMEM((8, 128), F32),
            pltpu.VMEM((8, 128), F32),
            pltpu.VMEM((1024, 128), F32),
            pltpu.VMEM((6, 384, 128), F32),
            pltpu.VMEM((2, 384, 768), BF),
            pltpu.SemaphoreType.DMA((4, 2)),
            pltpu.SemaphoreType.DMA((5, 2)),
            pltpu.SemaphoreType.DMA,
            pltpu.SemaphoreType.DMA((2,)),
            pltpu.SemaphoreType.DMA((2,)),
            pltpu.SemaphoreType.DMA((4,)),
            pltpu.SemaphoreType.DMA((4,)),
            pltpu.SemaphoreType.DMA((4,)),
            pltpu.SemaphoreType.DMA((2,)),
        ],
        compiler_params=pltpu.CompilerParams(
            collective_id=0, has_side_effects=True, vmem_limit_bytes=48 * 1024 * 1024),
    )(vol, wt, first_weight, second_weight, up_bias[None], first_bias[None], second_bias[None])
    return jnp.transpose(out, (2, 0, 1, 3))


def solution(mesh):
    placed = (P("filt", "depth", None), P(None, "filt"), P("filt"), P(), P(), P(), P())
    return jax.shard_map(
        functools.partial(shards, mesh.shape["depth"]),
        mesh=mesh,
        in_specs=placed,
        out_specs=P("filt", "depth", None, None),
        check_vma=False,
    )
```

```python
import functools

import jax
import jax.numpy as jnp
from jax import lax
from jax.experimental import pallas as pl
from jax.experimental.pallas import tpu as pltpu
from jax.sharding import PartitionSpec as P

BF = jnp.bfloat16
F32 = jnp.float32
MESH = pl.DeviceIdType.MESH


def shift_add(low, mid, high, lane):
    left = jnp.where(lane > 0, pltpu.roll(low, 1, 1), 0.0)
    right = jnp.where(lane < 127, pltpu.roll(high, 127, 1), 0.0)
    return mid + left + right


def conv_rows(src, weight, bias, places, lane):
    groups = []
    for plane, row in places:
        groups.append(jnp.concatenate([src[plane + kd, row + i] for kd in range(3) for i in range(4)], axis=0))
    total = jnp.dot(weight, jnp.concatenate(groups, axis=1), preferred_element_type=F32)
    outs = []
    for at in range(len(places)):
        cols = slice(128 * at, 128 * at + 128)
        for j in range(2):
            base = 192 * j
            value = shift_add(total[base:base + 64, cols], total[base + 64:base + 128, cols],
                              total[base + 128:base + 192, cols], lane)
            value = value + bias
            outs.append(jnp.maximum(value, 0.2 * value))
    return outs


def kernel(devices, vol, wt, w1, w2, bu, b1, b2, out,
           grid_in, moved, wup, ups, hid, result, bmine, bother, spread, packed, wconv,
           send, recv, xsend, wsend, wrecv, osend, orecv, lsem, bsem):
    d = lax.axis_index("depth")
    f = lax.axis_index("filt")
    g = 1 - f
    core = lax.rem(d, 2)
    s = 1 - 2 * core

    def exists(t):
        return jnp.logical_and(t >= 0, t < devices)

    barrier = pltpu.get_barrier_semaphore()
    pl.semaphore_signal(barrier, inc=1, device_id=(d, g), device_id_type=MESH)
    for off in (-2, -1, 1, 2):
        @pl.when(exists(d + off))
        def _():
            pl.semaphore_signal(barrier, inc=1, device_id=(d + off, f), device_id_type=MESH)
    peers = 1
    for off in (-2, -1, 1, 2):
        peers = peers + jnp.where(exists(d + off), 1, 0)
    pl.semaphore_wait(barrier, peers)

    x_copy = pltpu.make_async_remote_copy(
        src_ref=vol.at[:, pl.ds(pl.multiple_of(384 * g, 128), 640)],
        dst_ref=grid_in.at[2, f], send_sem=xsend, recv_sem=recv.at[2, f],
        device_id=(d, g), device_id_type=MESH)
    x_copy.start()
    w_half = pl.ds(8 * core, 8)
    w_copy = pltpu.make_async_remote_copy(
        src_ref=wt.at[w_half], dst_ref=wup.at[w_half, f], send_sem=wsend.at[0], recv_sem=wrecv.at[0],
        device_id=(d, g), device_id_type=MESH)
    w_copy.start()
    bmine[...] = jnp.zeros((8, 128), F32)
    bmine[0:1, 0:32] = bu[...]
    b_copy = pltpu.make_async_remote_copy(
        src_ref=bmine, dst_ref=bother, send_sem=bsem.at[0], recv_sem=bsem.at[1],
        device_id=(d, g), device_id_type=MESH)
    b_copy.start()
    grid_in[2, f] = vol[:, pl.ds(pl.multiple_of(384 * f, 128), 640)]

    def to_depth(half, which, at, target):
        slot = d - target + 2 if which < 3 else 2 - 2 * s
        return pltpu.make_async_remote_copy(
            src_ref=grid_in.at[at, half], dst_ref=grid_in.at[slot, half],
            send_sem=send.at[which, half], recv_sem=recv.at[slot, half],
            device_id=(target, f), device_id_type=MESH)

    def arrived(slot, half):
        pltpu.make_async_copy(grid_in.at[slot, half], grid_in.at[slot, half], recv.at[slot, half]).wait()

    def start_half(half, some):
        for which in some:
            off = (-s, s, 2 * s)[which]

            @pl.when(exists(d + off))
            def _():
                to_depth(half, which, 2, d + off).start()

    start_half(f, (0, 1))
    for off in (-2, -1, 1, 2):
        @pl.when(jnp.logical_not(exists(d + off)))
        def _():
            grid_in[2 + off] = jnp.zeros(grid_in.shape[1:], BF)
    for k in range(16):
        wup[k, f] = wt[k]
    ups[:, 0] = jnp.zeros((6, 64, 128), BF)
    ups[:, 21] = jnp.zeros((6, 64, 128), BF)
    hid[:, 0] = jnp.zeros((4, 64, 128), BF)
    hid[:, 19] = jnp.zeros((4, 64, 128), BF)

    lane_q = lax.broadcasted_iota(jnp.int32, (32, 128), 1)
    def rearrange(at, raw):
        for q in range(32):
            spread[32 * q:32 * q + 27, :] = raw[:, 128 * q:128 * q + 128].astype(F32)

        def tap_rows(e):
            return spread[pl.ds(e, 32, stride=32), :]

        nothing = jnp.zeros((32, 128), F32)
        for kw in range(3):
            for kd in range(3):
                rows_of = [tap_rows(9 * kd + 3 * kh + kw) for kh in range(3)]
                turned = [pltpu.roll(value, 64, 1) for value in rows_of]
                for j in range(2):
                    for pair in range(2):
                        m, base = 2 * kd + pair, 192 * j + 64 * kw
                        low, high = 2 * pair - j, 2 * pair + 1 - j
                        even = rows_of[low] if 0 <= low < 3 else nothing
                        odd_ = turned[high] if 0 <= high < 3 else nothing
                        packed[m, pl.ds(base, 32, stride=2), :] = jnp.where(lane_q < 64, even, odd_)
                        even = turned[low] if 0 <= low < 3 else nothing
                        odd_ = rows_of[high] if 0 <= high < 3 else nothing
                        packed[m, pl.ds(base + 1, 32, stride=2), :] = jnp.where(lane_q < 64, even, odd_)
        for m in range(6):
            wconv[at, :, 128 * m:128 * m + 128] = packed[m].astype(BF)

    rearrange(0, w1)

    x_recv = pltpu.make_async_copy(grid_in.at[2, g], grid_in.at[2, g], recv.at[2, g])
    x_recv.wait()
    start_half(g, (0, 1))

    rearrange(1, w2)

    def forward(half):
        @pl.when(exists(d - s))
        def _():
            arrived(2 - s, half)
            to_depth(half, 3, 2 - s, d + s).start()

    forward(f)
    forward(g)
    start_half(f, (2,))
    start_half(g, (2,))
    w_forward = pltpu.make_async_remote_copy(
        src_ref=wup.at[w_half, g], dst_ref=wup.at[w_half, g], send_sem=wsend.at[1], recv_sem=wrecv.at[1],
        device_id=(d + s, f), device_id_type=MESH)
    w_copy.wait_recv()
    w_forward.start()
    for half in range(2):
        arrived(2 + s, half)

    lane = lax.broadcasted_iota(jnp.int32, (64, 128), 1)
    lane_in = lax.broadcasted_iota(jnp.int32, (128, 128), 1)
    row_at = lax.broadcasted_iota(jnp.int32, (256, 256), 0)
    col_at = lax.broadcasted_iota(jnp.int32, (256, 256), 1)
    odd, rest = row_at // 128, row_at % 128
    place = jnp.where(col_at == 128 * (rest // 64) + 2 * (rest % 64) + odd, 1.0, 0.0).astype(BF)

    def column(row, count):
        at = lax.broadcasted_iota(jnp.int32, (count, count), 0)
        to = lax.broadcasted_iota(jnp.int32, (count, count), 1)
        return jnp.sum(jnp.where(at == to, row, 0.0), axis=1, keepdims=True)

    b_copy.wait_recv()
    mine, other = column(bmine[0:1, 0:32], 32), column(bother[0:1, 0:32], 32)
    bias_up = jnp.concatenate([jnp.where(f == 0, mine, other), jnp.where(f == 0, other, mine)], axis=0)
    bias_1, bias_2 = column(b1[...], 64), column(b2[...], 64)

    def shifted(slot):
        whole = grid_in[slot].reshape(128, 640).astype(F32)
        zero = jnp.zeros((128, 128), F32)
        turned = [zero] + [pltpu.roll(whole[:, 128 * t:128 * t + 128], 64, 1) for t in range(5)] + [zero]
        for t in range(6):
            moved[slot, :, 128 * t:128 * t + 128] = jnp.where(lane_in < 64, turned[t], turned[t + 1]).astype(BF)

    def upsample_plane(p):
        q, pd = p // 2, p % 2
        inside = exists(d - 1 + q)
        slots = (q + 1, q + 2 * pd)
        kds = (1 + pd, 3 - 3 * pd)
        for ph in range(2):
            khs = (1 + ph, 3 - 3 * ph)
            left, right = [], []
            for slot, kd in zip(slots, kds):
                for at, kh in enumerate(khs):
                    left.append(wup[4 * kd + kh].reshape(256, 128))
                    if at == 0:
                        right.append(grid_in[slot].reshape(128, 640))
                    else:
                        right.append(moved[slot, :, 128 * ph:128 * ph + 640])
            total = jnp.dot(jnp.concatenate(left, axis=1), jnp.concatenate(right, axis=0),
                            preferred_element_type=F32)
            rows = []
            for t in range(5):
                cols = slice(128 * t, 128 * t + 128)
                tap = [jnp.concatenate([total[32 * k:32 * k + 32, cols], total[128 + 32 * k:160 + 32 * k, cols]], axis=0)
                       for k in range(4)]
                even = tap[1] + jnp.where(lane % 64 > 0, pltpu.roll(tap[3], 1, 1), 0.0) + bias_up
                odd_ = tap[2] + jnp.where(lane % 64 < 63, pltpu.roll(tap[0], 127, 1), 0.0) + bias_up
                rows.append(jnp.concatenate([even, odd_], axis=1))
            both = jnp.where(inside, jnp.concatenate(rows, axis=0), 0.0).astype(BF)
            mixed = jnp.dot(both, place, preferred_element_type=F32).astype(BF)
            for t in range(5):
                for r in range(2):
                    ups[p, 1 + 2 * (2 * t + r) + ph] = mixed[64 * t:64 * t + 64, 128 * r:128 * r + 128]

    for slot in (1, 2, 3):
        shifted(slot)
    w_forward.wait_recv()
    lax.fori_loop(1, 5, lambda p, c: (upsample_plane(p), c)[1], 0)

    def hidden_pass(planes):
        def step(i, c):
            places, spots = [], []
            for r in range(6):
                group = 6 * i + r
                plane = planes[0] + (planes[1] - planes[0]) * (group // 9)
                row = 2 * (group % 9)
                places.append((plane, 2 * f + row))
                spots.append((plane, row))
            values = conv_rows(ups, wconv[0], bias_1, places, lane)
            for r, (plane, row) in enumerate(spots):
                at = 2 * d - 1 + plane
                inside = jnp.logical_and(at >= 0, at < 2 * devices)
                for j in range(2):
                    hid[plane, 1 + row + j] = jnp.where(inside, values[2 * r + j], 0.0).astype(BF)
            return c

        lax.fori_loop(0, 3, step, 0)

    hidden_pass((1, 2))

    for half in range(2):
        @pl.when(exists(d - 2 * s))
        def _():
            arrived(2 - 2 * s, half)

        @pl.when(exists(d + 2 * s))
        def _():
            arrived(2 + 2 * s, half)
    for slot in (0, 4):
        shifted(slot)
    lax.fori_loop(0, 2, lambda i, c: (upsample_plane(5 * i), c)[1], 0)
    hidden_pass((0, 3))

    def piece(k):
        return result.at[k // 2, :, pl.ds(8 * (k % 2), 8)], out.at[k // 2, pl.ds(16 * f + 8 * (k % 2), 8)]

    def out_copy(k):
        source, target = piece(k)
        return pltpu.make_async_remote_copy(
            src_ref=source.at[g], dst_ref=target,
            send_sem=osend.at[k], recv_sem=orecv.at[k], device_id=(d, g), device_id_type=MESH)

    def own_copy(k):
        source, target = piece(k)
        return pltpu.make_async_copy(source.at[f], target, lsem.at[k])

    for k in range(4):
        plane, row = k // 2, 8 * (k % 2)
        places = [(plane, 2 * f + row + 2 * r) for r in range(4)]
        for r, value in enumerate(conv_rows(hid, wconv[1], bias_2, places, lane)):
            value = value.astype(BF)
            result[plane, 0, row + r] = value[0:32]
            result[plane, 1, row + r] = value[32:64]
        out_copy(k).start()
        own_copy(k).start()

    b_copy.wait_send()
    x_copy.wait_send()
    w_copy.wait_send()
    w_forward.wait_send()
    for half in range(2):
        for which, off in enumerate((-s, s, 2 * s)):
            @pl.when(exists(d + off))
            def _():
                to_depth(half, which, 2, d + off).wait_send()

        @pl.when(exists(d - s))
        def _():
            to_depth(half, 3, 2 - s, d + s).wait_send()
    for k in range(4):
        own_copy(k).wait()
        out_copy(k).wait()


def shards(devices, volume, up_weight, up_bias, first_weight, first_bias, second_weight, second_bias):
    vol = volume.reshape(64, 1024)
    wt = jnp.transpose(up_weight.reshape(128, 32, 16, 4), (2, 3, 1, 0)).reshape(16, 128, 128)
    vmem = pl.BlockSpec(memory_space=pltpu.VMEM)
    out = pl.pallas_call(
        functools.partial(kernel, devices),
        out_shape=jax.ShapeDtypeStruct((2, 32, 32, 128), BF),
        in_specs=[vmem] * 7,
        out_specs=vmem,
        scratch_shapes=[
            pltpu.VMEM((5, 2, 64, 640), BF),
            pltpu.VMEM((5, 128, 768), BF),
            pltpu.VMEM((16, 2, 128, 128), BF),
            pltpu.VMEM((6, 22, 64, 128), BF),
            pltpu.VMEM((4, 20, 64, 128), BF),
            pltpu.VMEM((2, 2, 16, 32, 128), BF),
            pltpu.VMEM((8, 128), F32),
            pltpu.VMEM((8, 128), F32),
            pltpu.VMEM((1024, 128), F32),
            pltpu.VMEM((6, 384, 128), F32),
            pltpu.VMEM((2, 384, 768), BF),
            pltpu.SemaphoreType.DMA((4, 2)),
            pltpu.SemaphoreType.DMA((5, 2)),
            pltpu.SemaphoreType.DMA,
            pltpu.SemaphoreType.DMA((2,)),
            pltpu.SemaphoreType.DMA((2,)),
            pltpu.SemaphoreType.DMA((4,)),
            pltpu.SemaphoreType.DMA((4,)),
            pltpu.SemaphoreType.DMA((4,)),
            pltpu.SemaphoreType.DMA((2,)),
        ],
        compiler_params=pltpu.CompilerParams(
            collective_id=0, has_side_effects=True, vmem_limit_bytes=48 * 1024 * 1024),
    )(vol, wt, first_weight, second_weight, up_bias[None], first_bias[None], second_bias[None])
    return jnp.transpose(out, (2, 0, 1, 3))


def solution(mesh):
    placed = (P("filt", "depth", None), P(None, "filt"), P("filt"), P(), P(), P(), P())
    return jax.shard_map(
        functools.partial(shards, mesh.shape["depth"]),
        mesh=mesh,
        in_specs=placed,
        out_specs=P("filt", "depth", None, None),
        check_vma=False,
    )
```

```python
import functools

import jax
import jax.numpy as jnp
from jax import lax
from jax.experimental import pallas as pl
from jax.experimental.pallas import tpu as pltpu
from jax.sharding import PartitionSpec as P

BF = jnp.bfloat16
F32 = jnp.float32
MESH = pl.DeviceIdType.MESH


def shift_add(low, mid, high, lane):
    left = jnp.where(lane > 0, pltpu.roll(low, 1, 1), 0.0)
    right = jnp.where(lane < 127, pltpu.roll(high, 127, 1), 0.0)
    return mid + left + right


def conv_rows(src, weight, bias, places, lane):
    groups = []
    for plane, row in places:
        groups.append(jnp.concatenate([src[plane + kd, row + i] for kd in range(3) for i in range(4)], axis=0))
    total = jnp.dot(weight, jnp.concatenate(groups, axis=1), preferred_element_type=F32)
    outs = []
    for at in range(len(places)):
        cols = slice(128 * at, 128 * at + 128)
        for j in range(2):
            base = 192 * j
            value = shift_add(total[base:base + 64, cols], total[base + 64:base + 128, cols],
                              total[base + 128:base + 192, cols], lane)
            value = value + bias
            outs.append(jnp.maximum(value, 0.2 * value))
    return outs


def kernel(devices, vol, wt, w1, w2, bu, b1, b2, out,
           grid_in, moved, wup, ups, hid, result, bmine, bother, spread, packed, wconv,
           send, recv, xsend, wsend, wrecv, osend, orecv, lsem, bsem):
    d = lax.axis_index("depth")
    f = lax.axis_index("filt")
    g = 1 - f
    core = lax.rem(d, 2)
    s = 1 - 2 * core

    def exists(t):
        return jnp.logical_and(t >= 0, t < devices)

    barrier = pltpu.get_barrier_semaphore()
    pl.semaphore_signal(barrier, inc=1, device_id=(d, g), device_id_type=MESH)
    for off in (-2, -1, 1, 2):
        @pl.when(exists(d + off))
        def _():
            pl.semaphore_signal(barrier, inc=1, device_id=(d + off, f), device_id_type=MESH)
    peers = 1
    for off in (-2, -1, 1, 2):
        peers = peers + jnp.where(exists(d + off), 1, 0)
    pl.semaphore_wait(barrier, peers)

    x_copy = pltpu.make_async_remote_copy(
        src_ref=vol.at[:, pl.ds(pl.multiple_of(384 * g, 128), 640)],
        dst_ref=grid_in.at[2, f], send_sem=xsend, recv_sem=recv.at[2, f],
        device_id=(d, g), device_id_type=MESH)
    x_copy.start()
    w_half = pl.ds(8 * core, 8)
    w_copy = pltpu.make_async_remote_copy(
        src_ref=wt.at[w_half], dst_ref=wup.at[w_half, f], send_sem=wsend.at[0], recv_sem=wrecv.at[0],
        device_id=(d, g), device_id_type=MESH)
    w_copy.start()
    bmine[...] = jnp.zeros((8, 128), F32)
    bmine[0:1, 0:32] = bu[...]
    b_copy = pltpu.make_async_remote_copy(
        src_ref=bmine, dst_ref=bother, send_sem=bsem.at[0], recv_sem=bsem.at[1],
        device_id=(d, g), device_id_type=MESH)
    b_copy.start()
    grid_in[2, f] = vol[:, pl.ds(pl.multiple_of(384 * f, 128), 640)]

    def to_depth(half, which, at, target):
        slot = d - target + 2 if which < 3 else 2 - 2 * s
        return pltpu.make_async_remote_copy(
            src_ref=grid_in.at[at, half], dst_ref=grid_in.at[slot, half],
            send_sem=send.at[which, half], recv_sem=recv.at[slot, half],
            device_id=(target, f), device_id_type=MESH)

    def arrived(slot, half):
        pltpu.make_async_copy(grid_in.at[slot, half], grid_in.at[slot, half], recv.at[slot, half]).wait()

    def start_half(half, some):
        for which in some:
            off = (-s, s, 2 * s)[which]

            @pl.when(exists(d + off))
            def _():
                to_depth(half, which, 2, d + off).start()

    start_half(f, (0, 1))
    for off in (-2, -1, 1, 2):
        @pl.when(jnp.logical_not(exists(d + off)))
        def _():
            grid_in[2 + off] = jnp.zeros(grid_in.shape[1:], BF)
    for k in range(16):
        wup[k, f] = wt[k]
    ups[:, 0] = jnp.zeros((6, 64, 128), BF)
    ups[:, 21] = jnp.zeros((6, 64, 128), BF)
    hid[:, 0] = jnp.zeros((4, 64, 128), BF)
    hid[:, 19] = jnp.zeros((4, 64, 128), BF)

    lane_q = lax.broadcasted_iota(jnp.int32, (32, 128), 1)
    def rearrange(at, raw):
        for q in range(32):
            spread[32 * q:32 * q + 27, :] = raw[:, 128 * q:128 * q + 128].astype(F32)

        def tap_rows(e):
            return spread[pl.ds(e, 32, stride=32), :]

        nothing = jnp.zeros((32, 128), F32)
        for kw in range(3):
            for kd in range(3):
                rows_of = [tap_rows(9 * kd + 3 * kh + kw) for kh in range(3)]
                turned = [pltpu.roll(value, 64, 1) for value in rows_of]
                for j in range(2):
                    for pair in range(2):
                        m, base = 2 * kd + pair, 192 * j + 64 * kw
                        low, high = 2 * pair - j, 2 * pair + 1 - j
                        even = rows_of[low] if 0 <= low < 3 else nothing
                        odd_ = turned[high] if 0 <= high < 3 else nothing
                        packed[m, pl.ds(base, 32, stride=2), :] = jnp.where(lane_q < 64, even, odd_)
                        even = turned[low] if 0 <= low < 3 else nothing
                        odd_ = rows_of[high] if 0 <= high < 3 else nothing
                        packed[m, pl.ds(base + 1, 32, stride=2), :] = jnp.where(lane_q < 64, even, odd_)
        for m in range(6):
            wconv[at, :, 128 * m:128 * m + 128] = packed[m].astype(BF)

    rearrange(0, w1)

    x_recv = pltpu.make_async_copy(grid_in.at[2, g], grid_in.at[2, g], recv.at[2, g])
    x_recv.wait()
    start_half(g, (0, 1))

    rearrange(1, w2)

    def forward(half):
        @pl.when(exists(d - s))
        def _():
            arrived(2 - s, half)
            to_depth(half, 3, 2 - s, d + s).start()

    forward(f)
    forward(g)
    start_half(f, (2,))
    start_half(g, (2,))
    w_forward = pltpu.make_async_remote_copy(
        src_ref=wup.at[w_half, g], dst_ref=wup.at[w_half, g], send_sem=wsend.at[1], recv_sem=wrecv.at[1],
        device_id=(d + s, f), device_id_type=MESH)
    w_copy.wait_recv()
    w_forward.start()
    for half in range(2):
        arrived(2 + s, half)

    lane = lax.broadcasted_iota(jnp.int32, (64, 128), 1)
    lane_in = lax.broadcasted_iota(jnp.int32, (128, 128), 1)
    row_at = lax.broadcasted_iota(jnp.int32, (256, 256), 0)
    col_at = lax.broadcasted_iota(jnp.int32, (256, 256), 1)
    odd, rest = row_at // 128, row_at % 128
    place = jnp.where(col_at == 128 * (rest // 64) + 2 * (rest % 64) + odd, 1.0, 0.0).astype(BF)

    def column(row, count):
        at = lax.broadcasted_iota(jnp.int32, (count, count), 0)
        to = lax.broadcasted_iota(jnp.int32, (count, count), 1)
        return jnp.sum(jnp.where(at == to, row, 0.0), axis=1, keepdims=True)

    b_copy.wait_recv()
    mine, other = column(bmine[0:1, 0:32], 32), column(bother[0:1, 0:32], 32)
    bias_up = jnp.concatenate([jnp.where(f == 0, mine, other), jnp.where(f == 0, other, mine)], axis=0)
    bias_1, bias_2 = column(b1[...], 64), column(b2[...], 64)

    def shifted(slot):
        whole = grid_in[slot].reshape(128, 640).astype(F32)
        zero = jnp.zeros((128, 128), F32)
        turned = [zero] + [pltpu.roll(whole[:, 128 * t:128 * t + 128], 64, 1) for t in range(5)] + [zero]
        for t in range(6):
            moved[slot, :, 128 * t:128 * t + 128] = jnp.where(lane_in < 64, turned[t], turned[t + 1]).astype(BF)

    def upsample_plane(p):
        q, pd = p // 2, p % 2
        inside = exists(d - 1 + q)
        slots = (q + 1, q + 2 * pd)
        kds = (1 + pd, 3 - 3 * pd)
        for ph in range(2):
            khs = (1 + ph, 3 - 3 * ph)
            left, right = [], []
            for slot, kd in zip(slots, kds):
                for at, kh in enumerate(khs):
                    left.append(wup[4 * kd + kh].reshape(256, 128))
                    if at == 0:
                        right.append(grid_in[slot].reshape(128, 640))
                    else:
                        right.append(moved[slot, :, 128 * ph:128 * ph + 640])
            total = jnp.dot(jnp.concatenate(left, axis=1), jnp.concatenate(right, axis=0),
                            preferred_element_type=F32)
            rows = []
            for t in range(5):
                cols = slice(128 * t, 128 * t + 128)
                tap = [jnp.concatenate([total[32 * k:32 * k + 32, cols], total[128 + 32 * k:160 + 32 * k, cols]], axis=0)
                       for k in range(4)]
                even = tap[1] + jnp.where(lane % 64 > 0, pltpu.roll(tap[3], 1, 1), 0.0) + bias_up
                odd_ = tap[2] + jnp.where(lane % 64 < 63, pltpu.roll(tap[0], 127, 1), 0.0) + bias_up
                rows.append(jnp.concatenate([even, odd_], axis=1))
            both = jnp.where(inside, jnp.concatenate(rows, axis=0), 0.0).astype(BF)
            mixed = jnp.dot(both, place, preferred_element_type=F32).astype(BF)
            for t in range(5):
                for r in range(2):
                    ups[p, 1 + 2 * (2 * t + r) + ph] = mixed[64 * t:64 * t + 64, 128 * r:128 * r + 128]

    for slot in (1, 2, 3):
        shifted(slot)
    w_forward.wait_recv()
    lax.fori_loop(1, 5, lambda p, c: (upsample_plane(p), c)[1], 0, unroll=2)

    def hidden_pass(planes):
        def step(i, c):
            places, spots = [], []
            for r in range(6):
                group = 6 * i + r
                plane = planes[0] + (planes[1] - planes[0]) * (group // 9)
                row = 2 * (group % 9)
                places.append((plane, 2 * f + row))
                spots.append((plane, row))
            values = conv_rows(ups, wconv[0], bias_1, places, lane)
            for r, (plane, row) in enumerate(spots):
                at = 2 * d - 1 + plane
                inside = jnp.logical_and(at >= 0, at < 2 * devices)
                for j in range(2):
                    hid[plane, 1 + row + j] = jnp.where(inside, values[2 * r + j], 0.0).astype(BF)
            return c

        lax.fori_loop(0, 3, step, 0, unroll=True)

    hidden_pass((1, 2))

    for half in range(2):
        @pl.when(exists(d - 2 * s))
        def _():
            arrived(2 - 2 * s, half)

        @pl.when(exists(d + 2 * s))
        def _():
            arrived(2 + 2 * s, half)
    for slot in (0, 4):
        shifted(slot)
    lax.fori_loop(0, 2, lambda i, c: (upsample_plane(5 * i), c)[1], 0)
    hidden_pass((0, 3))

    def piece(k):
        return result.at[k // 2, :, pl.ds(8 * (k % 2), 8)], out.at[k // 2, pl.ds(16 * f + 8 * (k % 2), 8)]

    def out_copy(k):
        source, target = piece(k)
        return pltpu.make_async_remote_copy(
            src_ref=source.at[g], dst_ref=target,
            send_sem=osend.at[k], recv_sem=orecv.at[k], device_id=(d, g), device_id_type=MESH)

    def own_copy(k):
        source, target = piece(k)
        return pltpu.make_async_copy(source.at[f], target, lsem.at[k])

    for k in range(4):
        plane, row = k // 2, 8 * (k % 2)
        places = [(plane, 2 * f + row + 2 * r) for r in range(4)]
        for r, value in enumerate(conv_rows(hid, wconv[1], bias_2, places, lane)):
            value = value.astype(BF)
            result[plane, 0, row + r] = value[0:32]
            result[plane, 1, row + r] = value[32:64]
        out_copy(k).start()
        own_copy(k).start()

    b_copy.wait_send()
    x_copy.wait_send()
    w_copy.wait_send()
    w_forward.wait_send()
    for half in range(2):
        for which, off in enumerate((-s, s, 2 * s)):
            @pl.when(exists(d + off))
            def _():
                to_depth(half, which, 2, d + off).wait_send()

        @pl.when(exists(d - s))
        def _():
            to_depth(half, 3, 2 - s, d + s).wait_send()
    for k in range(4):
        own_copy(k).wait()
        out_copy(k).wait()


def shards(devices, volume, up_weight, up_bias, first_weight, first_bias, second_weight, second_bias):
    vol = volume.reshape(64, 1024)
    wt = jnp.transpose(up_weight.reshape(128, 32, 16, 4), (2, 3, 1, 0)).reshape(16, 128, 128)
    vmem = pl.BlockSpec(memory_space=pltpu.VMEM)
    out = pl.pallas_call(
        functools.partial(kernel, devices),
        out_shape=jax.ShapeDtypeStruct((2, 32, 32, 128), BF),
        in_specs=[vmem] * 7,
        out_specs=vmem,
        scratch_shapes=[
            pltpu.VMEM((5, 2, 64, 640), BF),
            pltpu.VMEM((5, 128, 768), BF),
            pltpu.VMEM((16, 2, 128, 128), BF),
            pltpu.VMEM((6, 22, 64, 128), BF),
            pltpu.VMEM((4, 20, 64, 128), BF),
            pltpu.VMEM((2, 2, 16, 32, 128), BF),
            pltpu.VMEM((8, 128), F32),
            pltpu.VMEM((8, 128), F32),
            pltpu.VMEM((1024, 128), F32),
            pltpu.VMEM((6, 384, 128), F32),
            pltpu.VMEM((2, 384, 768), BF),
            pltpu.SemaphoreType.DMA((4, 2)),
            pltpu.SemaphoreType.DMA((5, 2)),
            pltpu.SemaphoreType.DMA,
            pltpu.SemaphoreType.DMA((2,)),
            pltpu.SemaphoreType.DMA((2,)),
            pltpu.SemaphoreType.DMA((4,)),
            pltpu.SemaphoreType.DMA((4,)),
            pltpu.SemaphoreType.DMA((4,)),
            pltpu.SemaphoreType.DMA((2,)),
        ],
        compiler_params=pltpu.CompilerParams(
            collective_id=0, has_side_effects=True, vmem_limit_bytes=48 * 1024 * 1024),
    )(vol, wt, first_weight, second_weight, up_bias[None], first_bias[None], second_bias[None])
    return jnp.transpose(out, (2, 0, 1, 3))


def solution(mesh):
    placed = (P("filt", "depth", None), P(None, "filt"), P("filt"), P(), P(), P(), P())
    return jax.shard_map(
        functools.partial(shards, mesh.shape["depth"]),
        mesh=mesh,
        in_specs=placed,
        out_specs=P("filt", "depth", None, None),
        check_vma=False,
    )
```
